32 devices in a mesh: rep: 2 (over y), seq: 4 (over z), head: 2 (over x), sub: 2 (over core).
Axes of the slice: x: 2, y: 2, z: 4, core: 2. Of those that a mesh axis runs over, the one named last changes fastest.
Arguments:
- queries: bfloat16 [4096, 2048], P(('rep', 'seq', 'sub'), 'head'), parts along dimension 0, may hold values from -1.5 to 1.5
- key_vectors: bfloat16 [4096, 2048], P(('rep', 'seq'), 'head'), parts along dimension 0, may hold values from -1.5 to 1.5
- value_vectors: bfloat16 [4096, 2048], P(('rep', 'seq'), 'head'), parts along dimension 0, may hold values from -6 to 6
- gate_bins: int32 [4096, 16], P(('rep', 'seq'), 'head'), parts along dimension 0, may hold values from 0 to 2048
- doc_lengths: int32 [6], P('rep'), parts along dimension 0, may hold values from 1 to 1536, as said below
- decay_rates: float32 [16], P('head'), may hold values from 0.15 to 86
- ridge_terms: float32 [16], P('head'), may hold values from 0.5 to 2
Outputs:
- mesa_output: bfloat16 [4096, 2048], P(('rep', 'seq', 'sub'), 'head'), parts along dimension 0
The draws below stay inside these ranges and needn't reach their ends.
There are 2 independent parts, one for each index of `rep`. The reference program is written for one: setup_inputs(seed, part) draws one part's arguments, and reference() takes and returns one part's arrays. A program takes and returns all parts, laid end to end along the dimension named above; an argument that names none is the same for every part. Nothing has to cross between parts.
Inputs may be any that keep to these rules, and one draw needn't show every extreme that they name: `doc_lengths`: the lengths sum to 2048.
All inputs are finite; a program needn't handle non-finite values.
Results may differ from the reference program's by a relative error of at most 0.001.
Values sent between devices are 32-bit elements; how exact they have to be, the bound alone decides.
A program may use at most 64 MiB of HBM per device.

```python
import math
import jax
import jax.numpy as jnp
from jax import lax

H = 16
DK = 128
DV = 128
S_DEV = 512
ITERS = 4
INPUT_LENGTH = 2048


def document_layout(key):
    slot_key, split_key, run_key = jax.random.split(jax.random.fold_in(key, 51), 3)
    largest = INPUT_LENGTH * 3 // 4
    remainder = INPUT_LENGTH - largest
    largest_slot = jax.random.randint(slot_key, (), 0, 3, jnp.int32)
    first_other = jax.random.randint(split_key, (), 1, remainder, jnp.int32)
    second_other = (remainder - first_other).astype(jnp.int32)
    largest_len = jnp.full((), largest, jnp.int32)
    option_zero = jnp.stack([largest_len, first_other, second_other])
    option_one = jnp.stack([first_other, largest_len, second_other])
    option_two = jnp.stack([first_other, second_other, largest_len])
    doc_sizes = jnp.where(largest_slot == 0, option_zero, jnp.where(largest_slot == 1, option_one, option_two))
    largest_start = jnp.where(largest_slot == 0, 0, jnp.where(largest_slot == 1, first_other, first_other + second_other))
    run_offset = jax.random.randint(run_key, (), 1, INPUT_LENGTH // 2 + 1, jnp.int32)
    run_start = (largest_start + run_offset).astype(jnp.int32)
    return (doc_sizes.astype(jnp.int32), run_start)


def draw_doc_lengths(key, part):
    layout = document_layout(key)
    return layout[0]


def draw_key_vectors(key, part):
    leading_probe_vector, trailing_probe_vector = jax.random.split(jax.random.fold_in(key, 11))
    column_scales = jnp.exp(jax.random.uniform(leading_probe_vector, (H * DK,), jnp.float32, jnp.log(0.01), jnp.log(0.3)))
    lookup_cells = jnp.clip(jax.random.normal(trailing_probe_vector, (INPUT_LENGTH, H * DK), jnp.float32), -5.0, 5.0)
    return (lookup_cells * column_scales[None, :]).astype(jnp.bfloat16)


def draw_decay_rates(key, part):
    leading_probe_vector, trailing_probe_vector, third_key = jax.random.split(jax.random.fold_in(key, 23), 3)
    slow_rates = jnp.exp(jax.random.uniform(leading_probe_vector, (H,), jnp.float32, jnp.log(0.15), jnp.log(0.7)))
    fast_rates = jnp.exp(jax.random.uniform(trailing_probe_vector, (H,), jnp.float32, jnp.log(INPUT_LENGTH / 64.0), jnp.log(INPUT_LENGTH / 24.0)))
    slow_share = 0.5
    chosen = jax.random.uniform(third_key, (H,), jnp.float32) < slow_share
    return jnp.where(chosen, slow_rates, fast_rates).astype(jnp.float32)


def draw_gate_bins(key, part):
    layout = document_layout(key)
    run_start = layout[1]
    run_length = INPUT_LENGTH // 8
    bin_key, spike_key = jax.random.split(jax.random.fold_in(key, 37))
    lookup_cells = jax.random.randint(bin_key, (INPUT_LENGTH, H), 0, 3, jnp.int32)
    spike_draws = jax.random.randint(spike_key, (2,), 0, INPUT_LENGTH - 2 * run_length, jnp.int32)
    spike_indices = spike_draws + jnp.where(spike_draws >= run_start, 2 * run_length, 0).astype(jnp.int32)
    element_offsets = jnp.arange(INPUT_LENGTH, dtype=jnp.int32)
    spike_instances = jnp.any(element_offsets[:, None] == spike_indices[None, :], axis=1)
    in_run = (element_offsets >= run_start) & (element_offsets < run_start + run_length)
    binned = jnp.where(spike_instances[:, None], INPUT_LENGTH, lookup_cells)
    binned = jnp.where(in_run[:, None], 0, binned)
    return binned.astype(jnp.int32)


def block_scale(own_key, extent, cuts, low, top_value):
    factor_of, own = 1.0, jax.random.fold_in(own_key, 6)
    for axis_at, blocks in cuts:
        draws = jnp.exp(jax.random.uniform(jax.random.fold_in(own, axis_at), (blocks,), jnp.float32, low / len(cuts), top_value / len(cuts)))
        factor_of = factor_of * jnp.repeat(draws, extent[axis_at] // blocks).reshape([-1 if axis == axis_at else 1 for axis in range(len(extent))])
    return factor_of


def noise(rng, shape, scale, most, shards=(), kind=jnp.bfloat16):
    drawn = jax.random.normal(rng, shape, jnp.float32) * scale
    if len(shards) > 0:
        drawn = block_scale(rng, shape, shards, -0.22, 0.18) * drawn
    return jnp.clip(drawn, min=-most, max=most).astype(kind)


def setup_inputs(seed: int = 0, part: int = 0) -> dict:
    streams_of = jax.random.split(jax.random.key(seed), 8)
    part_splits = jax.random.split(jax.random.fold_in(streams_of[7], part), 8)
    return {
        "queries": noise(part_splits[0], (INPUT_LENGTH, H * DK), 0.25, 1.5, ((0, 8), (1, 2))),
        "key_vectors": draw_key_vectors(jax.random.fold_in(jax.random.fold_in(streams_of[7], part), 71), part),
        "value_vectors": noise(part_splits[2], (INPUT_LENGTH, H * DV), 1.0, 6.0, ((0, 4), (1, 2))),
        "gate_bins": draw_gate_bins(jax.random.fold_in(jax.random.fold_in(streams_of[7], part), 71), part),
        "doc_lengths": draw_doc_lengths(jax.random.fold_in(jax.random.fold_in(streams_of[7], part), 71), part),
        "decay_rates": draw_decay_rates(jax.random.fold_in(streams_of[7], 71), part),
        "ridge_terms": jnp.clip(jnp.exp(math.log(2.0) - 1.3862944 * jax.random.uniform(streams_of[6], (H,), jnp.float32) ** block_scale(streams_of[6], (H,), ((0, 2),), -0.2, 0.2)), 0.5, 2.0),
    }


highest = lax.Precision.HIGHEST
guard = 1e-6


def gate_weights(cumulative, doc_ids, query_cum, query_doc, query_pos, prior_doc):
    key_position = jnp.arange(cumulative.shape[0], dtype=jnp.int32)
    allowed = (key_position[None, :] <= query_pos[:, None]) & (doc_ids[None, :] == query_doc[:, None])
    spread_log = query_cum.T[:, :, None] - cumulative.T[:, None, :]
    weights = jnp.where(allowed[None], jnp.exp(jnp.minimum(spread_log, 0.0)), 0.0)
    carried = jnp.where((query_doc == prior_doc)[None, :], jnp.exp(query_cum.T), 0.0)
    return weights, carried


def solve_and_read(query_all, key_all, value_all, weights, carried, gram_state, memory, ridge_terms):
    def apply_system(direction):
        correlation = jnp.einsum('hrd,hsd->hrs', direction, key_all, precision=highest) * weights
        within = jnp.einsum('hrs,hsd->hrd', correlation, key_all, precision=highest)
        earlier = jnp.einsum('hrd,hed->hre', direction, gram_state, precision=highest)
        return carried[..., None] * earlier + within + ridge_terms[:, None, None] * direction

    solution = jnp.zeros_like(query_all)
    residual = query_all
    direction = query_all
    energy = jnp.sum(residual * residual, axis=-1)
    for iteration in range(ITERS):
        product = apply_system(direction)
        stepsize = energy / (jnp.sum(direction * product, axis=-1) + guard)
        solution = solution + stepsize[..., None] * direction
        residual = residual - stepsize[..., None] * product
        energy_next = jnp.sum(residual * residual, axis=-1)
        direction = residual + (energy_next / (energy + guard))[..., None] * direction
        energy = energy_next
    correlation = jnp.einsum('hrd,hsd->hrs', solution, key_all, precision=highest) * weights
    within = jnp.einsum('hrs,hse->hre', correlation, value_all, precision=highest)
    earlier = jnp.einsum('hrd,hed->hre', solution, memory, precision=highest)
    return carried[..., None] * earlier + within


def reference(queries, key_vectors, value_vectors, gate_bins, doc_lengths, decay_rates, ridge_terms):
    head_count = decay_rates.shape[0]
    key_width = key_vectors.shape[1] // head_count
    value_width = value_vectors.shape[1] // head_count
    block_count = INPUT_LENGTH // S_DEV
    doc_starts = (jnp.cumsum(doc_lengths, dtype=jnp.int32) - doc_lengths).astype(jnp.int32)
    element_offsets = jnp.arange(INPUT_LENGTH + 1, dtype=jnp.int32) - 1
    doc_all = jnp.sum((doc_starts[None, :] <= element_offsets[:, None]).astype(jnp.int32), axis=1, dtype=jnp.int32) - 1
    prior_docs = doc_all[:-1].reshape(block_count, S_DEV)[:, 0]
    doc_ids = doc_all[1:].reshape(block_count, S_DEV)
    log_gate = (-decay_rates[None, :] * gate_bins.astype(jnp.float32) / INPUT_LENGTH).reshape(block_count, S_DEV, head_count)

    def heads_first(array, width):
        return array.reshape(block_count, S_DEV, head_count, width).astype(jnp.float32).transpose(0, 2, 1, 3)

    query_all = heads_first(queries, key_width)
    key_all = heads_first(key_vectors, key_width)
    value_all = heads_first(value_vectors, value_width)

    def advance(state, inputs):
        gram_state, memory = state
        query_block, key_block, value_block, gate_block, doc_block, prior_doc = inputs
        cumulative = jnp.cumsum(gate_block, axis=0)
        query_pos = jnp.arange(S_DEV, dtype=jnp.int32)
        weights, carried = gate_weights(cumulative, doc_block, cumulative, doc_block, query_pos, prior_doc)
        output = solve_and_read(query_block, key_block, value_block, weights, carried, gram_state, memory, ridge_terms)
        end_weights = jnp.where((doc_block == doc_block[-1])[None, :], jnp.exp(cumulative[-1][:, None] - cumulative.T), 0.0)
        shard_decay = jnp.where(doc_block[-1] == prior_doc, jnp.exp(cumulative[-1]), 0.0)
        gram_sum = jnp.einsum('hsa,hsb->hab', key_block * end_weights[..., None], key_block, precision=highest)
        memory_sum = jnp.einsum('hsa,hsb->hab', value_block * end_weights[..., None], key_block, precision=highest)
        gram_state = shard_decay[:, None, None] * gram_state + gram_sum
        memory = shard_decay[:, None, None] * memory + memory_sum
        return (gram_state, memory), output

    start_state = (jnp.zeros((head_count, key_width, key_width), jnp.float32),
                   jnp.zeros((head_count, value_width, key_width), jnp.float32))
    unused, layer_results = lax.scan(advance, start_state, (query_all, key_all, value_all, log_gate, doc_ids, prior_docs))
    return layer_results.transpose(0, 2, 1, 3).reshape(INPUT_LENGTH, head_count * value_width).astype(jnp.bfloat16)
```

```python
import functools

import jax
import jax.numpy as jnp
from jax import lax
from jax.experimental import pallas as pl
from jax.experimental.pallas import tpu as pltpu
from jax.sharding import PartitionSpec as P

ITERS = 4
GUARD = 1e-06
FAR = 1e30
MESH = pl.DeviceIdType.MESH
f32 = jnp.float32
bf16 = jnp.bfloat16


def mm(a, b):
    return jnp.dot(a, b, preferred_element_type=f32)


def mm_t(a, b):
    return lax.dot_general(a, b, (((0,), (0,)), ((), ())), preferred_element_type=f32)


def split(x):
    hi = x.astype(bf16)
    return hi, (x - hi.astype(f32)).astype(bf16)


def kernel(
    seq_size, heads, rows, total_tokens,
    lengths_ref, rates_ref, ridge_ref, q_ref, k_ref, v_ref, bins_ref, out_ref,
    bcol, brow, penalty, gram_in, mem_in, gram_out, mem_out,
    sent_g, sent_m, got_g, got_m, pass_sg, pass_sm, pass_rg, pass_rm,
):
    shard = k_ref.shape[0]
    half = heads // 2
    width = 128
    me = lax.axis_index("seq")
    core = lax.axis_index("sub")
    row_start = pl.multiple_of(core * rows, rows)
    first = me * shard
    has_prev = me > 0
    has_next = me < seq_size - 1

    barrier = pltpu.get_barrier_semaphore()
    pl.semaphore_signal(barrier, inc=1, device_id={"sub": 1 - core}, device_id_type=MESH)

    @pl.when(has_prev)
    def _():
        pl.semaphore_signal(barrier, inc=1, device_id={"seq": me - 1}, device_id_type=MESH)

    @pl.when(has_next)
    def _():
        pl.semaphore_signal(barrier, inc=1, device_id={"seq": me + 1}, device_id_type=MESH)

    bins = bins_ref[...]
    high = (bins >> 7).astype(f32).astype(bf16)
    low = (bins & 127).astype(f32).astype(bf16)
    key_i = lax.broadcasted_iota(jnp.int32, (shard, shard), 0)
    key_j = lax.broadcasted_iota(jnp.int32, (shard, shard), 1)
    lower = jnp.where(key_i >= key_j, 1.0, 0.0).astype(bf16)
    upper = jnp.where(key_i <= key_j, 1.0, 0.0).astype(bf16)
    bcol[...] = 128.0 * mm(lower, high) + mm(lower, low)
    brow[...] = 128.0 * mm_t(high, upper) + mm_t(low, upper)

    starts = []
    start = jnp.int32(0)
    for d in range(lengths_ref.shape[0]):
        starts.append(start)
        start = start + lengths_ref[d]

    def doc_of(pos):
        count = jnp.zeros_like(pos)
        for s in starts:
            count = count + jnp.where(pos >= s, 1, 0)
        return count

    key_pos = lax.broadcasted_iota(jnp.int32, (1, shard), 1)
    key_doc = doc_of(first + key_pos)
    query_doc = doc_of(first + row_start + lax.broadcasted_iota(jnp.int32, (1, rows), 1))
    column_doc = doc_of(first + row_start + lax.broadcasted_iota(jnp.int32, (rows, 1), 0))
    one = jnp.zeros((1, 1), jnp.int32)
    prior_doc = doc_of(one + (first - 1))
    before_doc = doc_of(one + (first + row_start - 1))
    end_doc = doc_of(one + (first + shard - 1))
    si = lax.broadcasted_iota(jnp.int32, (rows, rows), 0)
    ti = lax.broadcasted_iota(jnp.int32, (rows, rows), 1)
    penalty[...] = jnp.where((si <= ti) & (column_doc == query_doc), 0.0, FAR)
    end_keep = jnp.where(key_doc == end_doc, 1.0, 0.0)
    shard_keep = jnp.where(end_doc == prior_doc, 1.0, 0.0)
    early_keep = jnp.where(
        (key_doc[:, :rows] == before_doc) & (key_pos[:, :rows] < row_start), 1.0, 0.0
    )
    start_keep = jnp.where(before_doc == prior_doc, 1.0, 0.0)
    carried_keep = jnp.where(query_doc == before_doc, 1.0, 0.0)
    later_core = jnp.where(one + core > 0, 1.0, 0.0)

    def rate_of(h):
        return rates_ref[h] * (-1.0 / total_tokens)

    def lanes(h):
        return pl.ds(pl.multiple_of(h * width, width), width)

    def chain_decay(h):
        return shard_keep * jnp.exp(rate_of(h) * brow[pl.ds(h, 1), :][:, shard - 1 :])

    def own_sums(i, carry):
        h = core * half + i
        sums = brow[pl.ds(h, 1), :]
        weight = end_keep * jnp.exp(rate_of(h) * (sums[:, shard - 1 : shard] - sums))
        keys = k_ref[:, lanes(h)]
        hi, lo = split(keys.T.astype(f32) * weight)
        both = jnp.concatenate([keys, v_ref[:, lanes(h)]], axis=1)
        total = mm(hi, both) + mm(lo, both)
        gram_out[i] = total[:, :width]
        mem_out[i] = total[:, width:]
        return carry

    lax.fori_loop(0, half, own_sums, 0)

    pl.semaphore_wait(
        barrier, 1 + jnp.where(has_prev, 1, 0) + jnp.where(has_next, 1, 0)
    )

    def forward(src, dst, sent, got, i):
        return pltpu.make_async_remote_copy(
            src_ref=src.at[i], dst_ref=dst.at[core * half + i],
            send_sem=sent.at[i], recv_sem=got.at[i],
            device_id={"seq": jnp.minimum(me + 1, seq_size - 1)}, device_id_type=MESH,
        )

    def across(buf, sent, got, i):
        h = core * half + i
        return pltpu.make_async_remote_copy(
            src_ref=buf.at[h], dst_ref=buf.at[h],
            send_sem=sent.at[i], recv_sem=got.at[i],
            device_id={"sub": 1 - core}, device_id_type=MESH,
        )

    def across_in(buf, sent, got, i):
        h = (1 - core) * half + i
        return pltpu.make_async_remote_copy(
            src_ref=buf.at[h], dst_ref=buf.at[h],
            send_sem=sent.at[i], recv_sem=got.at[i],
            device_id={"sub": 1 - core}, device_id_type=MESH,
        )

    def chain_step(src, buf, sent, got, pass_s, pass_r, i):
        h = core * half + i

        @pl.when(has_prev)
        def _():
            pltpu.make_async_remote_copy(
                src_ref=src.at[i], dst_ref=buf.at[h],
                send_sem=sent.at[i], recv_sem=got.at[i],
                device_id={"seq": jnp.maximum(me - 1, 0)}, device_id_type=MESH,
            ).wait_recv()
            across(buf, pass_s, pass_r, i).start()

            @pl.when(has_next)
            def _():
                src[i] = chain_decay(h) * buf[h] + src[i]

        @pl.when(has_next)
        def _():
            forward(src, buf, sent, got, i).start()

    def gram_step(i, carry):
        chain_step(gram_out, gram_in, sent_g, got_g, pass_sg, pass_rg, i)
        return carry

    @pl.when(jnp.logical_not(has_prev))
    def _():
        gram_in[...] = jnp.zeros_like(gram_in)
        mem_in[...] = jnp.zeros_like(mem_in)

    lax.fori_loop(0, half, gram_step, 0)

    head_lane = lax.broadcasted_iota(jnp.int32, (rows, heads), 1)

    def pair(i, carry):
        @pl.when(has_prev)
        def _():
            across_in(gram_in, pass_sg, pass_rg, i).wait_recv()

        group = (i, half + i)
        state = []
        for h in group:
            rate = rate_of(h)
            sums = brow[pl.ds(h, 1), :]
            query_sums = jnp.where(core > 0, sums[:, shard - rows :], sums[:, :rows])
            before = later_core * sums[:, rows - 1 : rows]
            column = jnp.sum(
                jnp.where(head_lane == h, bcol[pl.ds(row_start, rows), :], 0.0),
                axis=1, keepdims=True,
            )
            weights = jnp.exp(rate * (query_sums - column) - penalty[...])
            carried = carried_keep * jnp.exp(rate * (query_sums - before))
            decay = start_keep * jnp.exp(rate * before)
            early = early_keep * jnp.exp(
                rate * jnp.maximum(before - sums[:, :rows], 0.0)
            )
            old_keys = k_ref[0:rows, lanes(h)]
            hi, lo = split(old_keys.T.astype(f32) * early)
            both = jnp.concatenate([old_keys, v_ref[0:rows, lanes(h)]], axis=1)
            local = mm(hi, both) + mm(lo, both)
            ghi, glo = split(decay * gram_in[h] + local[:, :width])
            keys = k_ref[pl.ds(row_start, rows), lanes(h)]
            left = jnp.concatenate(
                [
                    jnp.concatenate([keys, keys], axis=1),
                    jnp.concatenate([ghi, ghi], axis=1),
                    jnp.concatenate([glo, glo], axis=1),
                ],
                axis=0,
            )
            query = q_ref[:, lanes(h)].T.astype(f32)
            state.append(
                dict(
                    weights=weights, carried=carried, decay=decay, mem=local[:, width:],
                    left=left, keys=keys, keys_t=keys.T, ridge=ridge_ref[h],
                    x=jnp.zeros_like(query), r=query, p=query,
                    energy=jnp.sum(query * query, axis=0, keepdims=True),
                )
            )
        for iteration in range(ITERS):
            for s in state:
                hi, lo = split(s["p"])
                s["y"] = mm(s["left"], jnp.concatenate([hi, lo], axis=0))
            for s in state:
                hi, lo = split(s["y"][:rows] * s["weights"])
                a = mm(s["keys_t"], hi) + mm(s["keys_t"], lo)
                earlier = s["y"][rows : rows + width] + s["y"][rows + width :]
                s["a"] = s["carried"] * earlier + a + s["ridge"] * s["p"]
            for s in state:
                p, a = s["p"], s["a"]
                alpha = s["energy"] / (jnp.sum(p * a, axis=0, keepdims=True) + GUARD)
                s["x"] = s["x"] + alpha * p
                if iteration < ITERS - 1:
                    r = s["r"] - alpha * a
                    energy = jnp.sum(r * r, axis=0, keepdims=True)
                    s["p"] = r + (energy / (s["energy"] + GUARD)) * p
                    s["r"], s["energy"] = r, energy

        chain_step(mem_out, mem_in, sent_m, got_m, pass_sm, pass_rm, i)
        within = []
        for h, s in zip(group, state):
            hi, lo = split(s["x"])
            s["hilo"] = jnp.concatenate([hi, lo], axis=0)
            keys2 = s["left"][:rows]
            hi, lo = split(mm(keys2, s["hilo"]) * s["weights"])
            values_t = v_ref[pl.ds(row_start, rows), lanes(h)].T
            within.append(mm(values_t, hi) + mm(values_t, lo))

        @pl.when(has_prev)
        def _():
            across_in(mem_in, pass_sm, pass_rm, i).wait_recv()

        for h, s, inner in zip(group, state, within):
            mhi, mlo = split((s["decay"] * mem_in[h] + s["mem"]).T)
            left = jnp.concatenate(
                [
                    jnp.concatenate([mhi, mhi], axis=1),
                    jnp.concatenate([mlo, mlo], axis=1),
                ],
                axis=0,
            )
            y = mm(left, s["hilo"])
            out = s["carried"] * (y[:width] + y[width:]) + inner
            out_ref[:, lanes(h)] = out.T.astype(bf16)
        return carry

    lax.fori_loop(0, half, pair, 0)

    def finish(i, carry):
        @pl.when(has_prev)
        def _():
            across(gram_in, pass_sg, pass_rg, i).wait_send()
            across(mem_in, pass_sm, pass_rm, i).wait_send()

        @pl.when(has_next)
        def _():
            forward(gram_out, gram_in, sent_g, got_g, i).wait_send()
            forward(mem_out, mem_in, sent_m, got_m, i).wait_send()

        return carry

    lax.fori_loop(0, half, finish, 0)


def per_device(seq_size, queries, keys, values, gate_bins, doc_lengths, decay_rates, ridge_terms):
    heads = decay_rates.shape[0]
    rows = queries.shape[0]
    shard = keys.shape[0]
    half = heads // 2
    width = keys.shape[1] // heads
    smem = pl.BlockSpec(memory_space=pltpu.SMEM)
    vmem = pl.BlockSpec(memory_space=pltpu.VMEM)
    flops = 2 * heads * rows * 256 * 768 * 5
    return pl.pallas_call(
        functools.partial(kernel, seq_size, heads, rows, shard * seq_size),
        out_shape=jax.ShapeDtypeStruct(queries.shape, bf16),
        in_specs=[smem, smem, smem, vmem, vmem, vmem, vmem],
        out_specs=vmem,
        scratch_shapes=[
            pltpu.VMEM((shard, heads), f32),
            pltpu.VMEM((heads, shard), f32),
            pltpu.VMEM((rows, rows), f32),
            pltpu.VMEM((heads, width, width), f32),
            pltpu.VMEM((heads, width, width), f32),
            pltpu.VMEM((half, width, width), f32),
            pltpu.VMEM((half, width, width), f32),
        ] + [pltpu.SemaphoreType.DMA((half,))] * 8,
        compiler_params=pltpu.CompilerParams(
            collective_id=0, has_side_effects=True, vmem_limit_bytes=48 * 1024 * 1024
        ),
        cost_estimate=pl.CostEstimate(
            flops=flops, bytes_accessed=4 * 1024 * 1024, transcendentals=heads * rows * rows
        ),
    )(doc_lengths, decay_rates, ridge_terms, queries, keys, values, gate_bins)


def solution(mesh):
    in_specs = (
        P(("rep", "seq", "sub"), "head"),
        P(("rep", "seq"), "head"),
        P(("rep", "seq"), "head"),
        P(("rep", "seq"), "head"),
        P("rep"),
        P("head"),
        P("head"),
    )
    out_specs = P(("rep", "seq", "sub"), "head")
    return jax.shard_map(
        functools.partial(per_device, mesh.shape["seq"]),
        mesh=mesh, in_specs=in_specs, out_specs=out_specs, check_vma=False,
    )
```

```python
import functools

import jax
import jax.numpy as jnp
from jax import lax
from jax.experimental import pallas as pl
from jax.experimental.pallas import tpu as pltpu
from jax.sharding import PartitionSpec as P

ITERS = 4
GUARD = 1e-06
FAR = 1e30
MESH = pl.DeviceIdType.MESH
f32 = jnp.float32
bf16 = jnp.bfloat16


def mm(a, b):
    return jnp.dot(a, b, preferred_element_type=f32)


def mm_nt(a, b):
    return lax.dot_general(a, b, (((1,), (1,)), ((), ())), preferred_element_type=f32)


def split(x):
    hi = x.astype(bf16)
    return hi, (x - hi.astype(f32)).astype(bf16)


def kernel(
    seq_size, heads, rows, total_tokens,
    lengths_ref, rates_ref, ridge_ref, q_hbm, k_hbm, v_hbm, bins_hbm, out_ref,
    q_ref, k_ref, v_ref, bins_ref,
    bcol, brow, penalty, gram_in, mem_in, gram_out, mem_out,
    weight_s, local_g, local_m, keys_ts, values_ts, query_ts,
    sent_g, sent_m, got_g, got_m, pass_sg, pass_sm, pass_rg, pass_rm, load_sem,
):
    shard = k_ref.shape[0]
    half = heads // 2
    width = 128
    me = lax.axis_index("seq")
    core = lax.axis_index("sub")
    row_start = pl.multiple_of(core * rows, rows)
    first = me * shard
    has_prev = me > 0
    has_next = me < seq_size - 1

    loads = [(bins_hbm, bins_ref)]
    piece = shard // 4
    for src, dst in ((k_hbm, k_ref), (v_hbm, v_ref), (q_hbm, q_ref)):
        for at in range(0, src.shape[0], piece):
            loads.append((src.at[pl.ds(at, piece)], dst.at[pl.ds(at, piece)]))
    loads = [
        pltpu.make_async_copy(src, dst, load_sem.at[at]) for at, (src, dst) in enumerate(loads)
    ]
    for load in loads:
        load.start()

    barrier = pltpu.get_barrier_semaphore()
    pl.semaphore_signal(barrier, inc=1, device_id={"sub": 1 - core}, device_id_type=MESH)

    @pl.when(has_prev)
    def _():
        pl.semaphore_signal(barrier, inc=1, device_id={"seq": me - 1}, device_id_type=MESH)

    @pl.when(has_next)
    def _():
        pl.semaphore_signal(barrier, inc=1, device_id={"seq": me + 1}, device_id_type=MESH)

    loads[0].wait()
    bins = bins_ref[...]
    high = (bins >> 7).astype(f32).astype(bf16)
    low = (bins & 127).astype(f32).astype(bf16)
    key_i = lax.broadcasted_iota(jnp.int32, (shard, shard), 0)
    key_j = lax.broadcasted_iota(jnp.int32, (shard, shard), 1)
    lower = jnp.where(key_i >= key_j, 1.0, 0.0).astype(bf16)
    upper = jnp.where(key_i <= key_j, 1.0, 0.0).astype(bf16)
    bcol[...] = 128.0 * mm_nt(lower, high) + mm_nt(lower, low)
    brow[...] = 128.0 * mm(high, upper) + mm(low, upper)

    starts = []
    start = jnp.int32(0)
    for d in range(lengths_ref.shape[0]):
        starts.append(start)
        start = start + lengths_ref[d]

    def doc_of(pos):
        count = jnp.zeros_like(pos)
        for s in starts:
            count = count + jnp.where(pos >= s, 1, 0)
        return count

    key_pos = lax.broadcasted_iota(jnp.int32, (1, shard), 1)
    key_doc = doc_of(first + key_pos)
    query_doc = doc_of(first + row_start + lax.broadcasted_iota(jnp.int32, (1, rows), 1))
    column_doc = doc_of(first + row_start + lax.broadcasted_iota(jnp.int32, (rows, 1), 0))
    one = jnp.zeros((1, 1), jnp.int32)
    prior_doc = doc_of(one + (first - 1))
    before_doc = doc_of(one + (first + row_start - 1))
    end_doc = doc_of(one + (first + shard - 1))
    si = lax.broadcasted_iota(jnp.int32, (rows, rows), 0)
    ti = lax.broadcasted_iota(jnp.int32, (rows, rows), 1)
    penalty[...] = jnp.where((si <= ti) & (column_doc == query_doc), 0.0, FAR)
    end_keep = jnp.where(key_doc == end_doc, 1.0, 0.0)
    shard_keep = jnp.where(end_doc == prior_doc, 1.0, 0.0)
    early_keep = jnp.where(
        (key_doc[:, :rows] == before_doc) & (key_pos[:, :rows] < row_start), 1.0, 0.0
    )
    start_keep = jnp.where(before_doc == prior_doc, 1.0, 0.0)
    carried_keep = jnp.where(query_doc == before_doc, 1.0, 0.0)
    later_core = jnp.where(one + core > 0, 1.0, 0.0)

    def rate_of(h):
        return rates_ref[h] * (-1.0 / total_tokens)

    def lanes(h):
        return pl.ds(pl.multiple_of(h * width, width), width)

    def chain_decay(h):
        return shard_keep * jnp.exp(rate_of(h) * brow[pl.ds(h, 1), :][:, shard - 1 :])

    def forward(src, dst, sent, got, i):
        return pltpu.make_async_remote_copy(
            src_ref=src.at[i], dst_ref=dst.at[core * half + i],
            send_sem=sent.at[i], recv_sem=got.at[i],
            device_id={"seq": jnp.minimum(me + 1, seq_size - 1)}, device_id_type=MESH,
        )

    def across(buf, sent, got, i):
        h = core * half + i
        return pltpu.make_async_remote_copy(
            src_ref=buf.at[h], dst_ref=buf.at[h],
            send_sem=sent.at[i], recv_sem=got.at[i],
            device_id={"sub": 1 - core}, device_id_type=MESH,
        )

    def across_in(buf, sent, got, i):
        h = (1 - core) * half + i
        return pltpu.make_async_remote_copy(
            src_ref=buf.at[h], dst_ref=buf.at[h],
            send_sem=sent.at[i], recv_sem=got.at[i],
            device_id={"sub": 1 - core}, device_id_type=MESH,
        )

    def own_sums(i, carry):
        h = core * half + i
        sums = brow[pl.ds(h, 1), :]
        weight = end_keep * jnp.exp(rate_of(h) * (sums[:, shard - 1 :] - sums))
        keys = k_ref[:, lanes(h)]
        hi, lo = split(keys.T.astype(f32) * weight)
        both = jnp.concatenate([keys, v_ref[:, lanes(h)]], axis=1)
        total = mm(hi, both) + mm(lo, both)
        gram_out[i] = total[:, :width]
        mem_out[i] = total[:, width:]

        @pl.when(jnp.logical_not(has_prev) & has_next)
        def _():
            forward(gram_out, gram_in, sent_g, got_g, i).start()
            forward(mem_out, mem_in, sent_m, got_m, i).start()

        return carry

    def chain_step(src, buf, sent, got, pass_s, pass_r, i):
        h = core * half + i

        @pl.when(has_prev)
        def _():
            pltpu.make_async_remote_copy(
                src_ref=src.at[i], dst_ref=buf.at[h],
                send_sem=sent.at[i], recv_sem=got.at[i],
                device_id={"seq": jnp.maximum(me - 1, 0)}, device_id_type=MESH,
            ).wait_recv()

            @pl.when(has_next)
            def _():
                src[i] = chain_decay(h) * buf[h] + src[i]
                forward(src, buf, sent, got, i).start()

            across(buf, pass_s, pass_r, i).start()

    def gram_step(i):
        chain_step(gram_out, gram_in, sent_g, got_g, pass_sg, pass_rg, i)

    def mem_step(i):
        chain_step(mem_out, mem_in, sent_m, got_m, pass_sm, pass_rm, i)

    @pl.when(jnp.logical_not(has_prev))
    def _():
        gram_in[...] = jnp.zeros_like(gram_in)
        mem_in[...] = jnp.zeros_like(mem_in)

    pl.semaphore_wait(
        barrier, 1 + jnp.where(has_prev, 1, 0) + jnp.where(has_next, 1, 0)
    )
    for load in loads[1:]:
        load.wait()
    lax.fori_loop(0, half, own_sums, 0)

    head_lane = lax.broadcasted_iota(jnp.int32, (rows, heads), 1)

    def query_sums_of(h):
        sums = brow[pl.ds(h, 1), :]
        query_sums = jnp.where(core > 0, sums[:, shard - rows :], sums[:, :rows])
        before = later_core * sums[:, rows - 1 : rows]
        return sums, query_sums, before

    def prepare(i):
        for h in (i, half + i):
            rate = rate_of(h)
            sums, query_sums, before = query_sums_of(h)
            column = jnp.sum(
                jnp.where(head_lane == h, bcol[pl.ds(row_start, rows), :], 0.0),
                axis=1, keepdims=True,
            )
            weight_s[h] = jnp.exp(rate * (query_sums - column) - penalty[...])
            early = early_keep * jnp.exp(
                rate * jnp.maximum(before - sums[:, :rows], 0.0)
            )
            old_keys = k_ref[0:rows, lanes(h)]
            hi, lo = split(old_keys.T.astype(f32) * early)
            both = jnp.concatenate([old_keys, v_ref[0:rows, lanes(h)]], axis=1)
            local = mm(hi, both) + mm(lo, both)
            local_g[h] = local[:, :width]
            local_m[h] = local[:, width:]
            keys_ts[h] = k_ref[pl.ds(row_start, rows), lanes(h)].T
            values_ts[h] = v_ref[pl.ds(row_start, rows), lanes(h)].T
            query_ts[h] = q_ref[:, lanes(h)].T

    ahead = jnp.minimum(half, me * 2)

    def prepare_ahead(i, carry):
        prepare(i)
        return carry

    lax.fori_loop(0, ahead, prepare_ahead, 0)
    gram_step(0)

    def pair(i, carry):
        @pl.when(i >= ahead)
        def _():
            prepare(i)

        @pl.when(has_prev)
        def _():
            across_in(gram_in, pass_sg, pass_rg, i).wait_recv()

        group = (i, half + i)
        state = []
        for h in group:
            rate = rate_of(h)
            sums, query_sums, before = query_sums_of(h)
            carried = carried_keep * jnp.exp(rate * (query_sums - before))
            decay = start_keep * jnp.exp(rate * before)
            ghi, glo = split(decay * gram_in[h] + local_g[h])
            keys = k_ref[pl.ds(row_start, rows), lanes(h)]
            left = jnp.concatenate(
                [
                    jnp.concatenate([keys, keys], axis=1),
                    jnp.concatenate([ghi, ghi], axis=1),
                    jnp.concatenate([glo, glo], axis=1),
                ],
                axis=0,
            )
            query = query_ts[h].astype(f32)
            state.append(
                dict(
                    h=h, carried=carried, decay=decay,
                    left=left, ridge=ridge_ref[h],
                    x=jnp.zeros_like(query), r=query, p=query,
                    energy=jnp.sum(query * query, axis=0, keepdims=True),
                )
            )
        for iteration in range(ITERS):
            for s in state:
                hi, lo = split(s["p"])
                s["y"] = mm(s["left"], jnp.concatenate([hi, lo], axis=0))
            for s in state:
                hi, lo = split(s["y"][:rows] * weight_s[s["h"]])
                a = mm(keys_ts[s["h"]], hi) + mm(keys_ts[s["h"]], lo)
                earlier = s["y"][rows : rows + width] + s["y"][rows + width :]
                s["a"] = s["carried"] * earlier + a + s["ridge"] * s["p"]
            for s in state:
                p, a = s["p"], s["a"]
                alpha = s["energy"] / (jnp.sum(p * a, axis=0, keepdims=True) + GUARD)
                s["x"] = s["x"] + alpha * p
                if iteration < ITERS - 1:
                    r = s["r"] - alpha * a
                    energy = jnp.sum(r * r, axis=0, keepdims=True)
                    s["p"] = r + (energy / (s["energy"] + GUARD)) * p
                    s["r"], s["energy"] = r, energy
            if iteration == 1:
                mem_step(i)

        @pl.when(i < half - 1)
        def _():
            gram_step(i + 1)

        within = []
        for h, s in zip(group, state):
            hi, lo = split(s["x"])
            s["hilo"] = jnp.concatenate([hi, lo], axis=0)
            keys2 = s["left"][:rows]
            hi, lo = split(mm(keys2, s["hilo"]) * weight_s[h])
            within.append(mm(values_ts[h], hi) + mm(values_ts[h], lo))

        @pl.when(has_prev)
        def _():
            across_in(mem_in, pass_sm, pass_rm, i).wait_recv()

        for h, s, inner in zip(group, state, within):
            mhi, mlo = split((s["decay"] * mem_in[h] + local_m[h]).T)
            left = jnp.concatenate(
                [
                    jnp.concatenate([mhi, mhi], axis=1),
                    jnp.concatenate([mlo, mlo], axis=1),
                ],
                axis=0,
            )
            y = mm(left, s["hilo"])
            out = s["carried"] * (y[:width] + y[width:]) + inner
            out_ref[:, lanes(h)] = out.T.astype(bf16)
        return carry

    lax.fori_loop(0, half, pair, 0)

    def finish(i, carry):
        @pl.when(has_prev)
        def _():
            across(gram_in, pass_sg, pass_rg, i).wait_send()
            across(mem_in, pass_sm, pass_rm, i).wait_send()

        @pl.when(has_next)
        def _():
            forward(gram_out, gram_in, sent_g, got_g, i).wait_send()
            forward(mem_out, mem_in, sent_m, got_m, i).wait_send()

        return carry

    lax.fori_loop(0, half, finish, 0)


def per_device(seq_size, queries, keys, values, gate_bins, doc_lengths, decay_rates, ridge_terms):
    heads = decay_rates.shape[0]
    rows = queries.shape[0]
    shard = keys.shape[0]
    half = heads // 2
    width = keys.shape[1] // heads
    smem = pl.BlockSpec(memory_space=pltpu.SMEM)
    vmem = pl.BlockSpec(memory_space=pltpu.VMEM)
    hbm = pl.BlockSpec(memory_space=pltpu.HBM)
    square = pltpu.VMEM((heads, width, width), f32)
    turned = pltpu.VMEM((heads, width, rows), bf16)
    flops = 2 * heads * rows * 256 * 768 * 5
    return pl.pallas_call(
        functools.partial(kernel, seq_size, heads, rows, shard * seq_size),
        out_shape=jax.ShapeDtypeStruct(queries.shape, bf16),
        in_specs=[smem, smem, smem, hbm, hbm, hbm, hbm],
        out_specs=vmem,
        scratch_shapes=[
            pltpu.VMEM(queries.shape, bf16),
            pltpu.VMEM(keys.shape, bf16),
            pltpu.VMEM(values.shape, bf16),
            pltpu.VMEM((heads, shard), jnp.int32),
            pltpu.VMEM((shard, heads), f32),
            pltpu.VMEM((heads, shard), f32),
            pltpu.VMEM((rows, rows), f32),
            square, square,
            pltpu.VMEM((half, width, width), f32),
            pltpu.VMEM((half, width, width), f32),
            pltpu.VMEM((heads, rows, rows), f32),
            square, square, turned, turned, turned,
        ] + [pltpu.SemaphoreType.DMA((half,))] * 8 + [pltpu.SemaphoreType.DMA((16,))],
        compiler_params=pltpu.CompilerParams(
            collective_id=0, has_side_effects=True, vmem_limit_bytes=62 * 1024 * 1024
        ),
        cost_estimate=pl.CostEstimate(
            flops=flops, bytes_accessed=4 * 1024 * 1024, transcendentals=heads * rows * rows
        ),
    )(doc_lengths, decay_rates, ridge_terms, queries, keys, values, gate_bins.T)


def solution(mesh):
    in_specs = (
        P(("rep", "seq", "sub"), "head"),
        P(("rep", "seq"), "head"),
        P(("rep", "seq"), "head"),
        P(("rep", "seq"), "head"),
        P("rep"),
        P("head"),
        P("head"),
    )
    out_specs = P(("rep", "seq", "sub"), "head")
    return jax.shard_map(
        functools.partial(per_device, mesh.shape["seq"]),
        mesh=mesh, in_specs=in_specs, out_specs=out_specs, check_vma=False,
    )
```

```python
import functools

import jax
import jax.numpy as jnp
from jax import lax
from jax.experimental import pallas as pl
from jax.experimental.pallas import tpu as pltpu
from jax.sharding import PartitionSpec as P

ITERS = 4
GUARD = 1e-06
FAR = 1e30
MESH = pl.DeviceIdType.MESH
f32 = jnp.float32
bf16 = jnp.bfloat16


def mm(a, b):
    return jnp.dot(a, b, preferred_element_type=f32)


def mm_nt(a, b):
    return lax.dot_general(a, b, (((1,), (1,)), ((), ())), preferred_element_type=f32)


def split(x):
    hi = x.astype(bf16)
    return hi, (x - hi.astype(f32)).astype(bf16)


def kernel(
    seq_size, heads, rows, total_tokens,
    lengths_ref, rates_ref, ridge_ref, q_hbm, k_hbm, v_hbm, bins_hbm, out_ref,
    q_ref, k_ref, v_ref, bins_ref,
    bcol, brow, penalty, came, flow,
    weight_s, local_g, local_m, keys_ts, values_ts, query_ts,
    sent, got, pass_s, pass_r, load_sem,
):
    shard = k_ref.shape[0]
    half = heads // 2
    width = came.shape[3]
    steps = flow.shape[0]
    me = lax.axis_index("seq")
    core = lax.axis_index("sub")
    row_start = pl.multiple_of(core * rows, rows)
    first = me * shard
    has_prev = me > 0
    has_next = me < seq_size - 1

    loads = [(bins_hbm, bins_ref)]
    piece = shard // 4
    for src, dst in ((k_hbm, k_ref), (v_hbm, v_ref), (q_hbm, q_ref)):
        for at in range(0, src.shape[0], piece):
            loads.append((src.at[pl.ds(at, piece)], dst.at[pl.ds(at, piece)]))
    loads = [
        pltpu.make_async_copy(src, dst, load_sem.at[at]) for at, (src, dst) in enumerate(loads)
    ]
    for load in loads:
        load.start()

    barrier = pltpu.get_barrier_semaphore()
    pl.semaphore_signal(barrier, inc=1, device_id={"sub": 1 - core}, device_id_type=MESH)

    @pl.when(has_prev)
    def _():
        pl.semaphore_signal(barrier, inc=1, device_id={"seq": me - 1}, device_id_type=MESH)

    @pl.when(has_next)
    def _():
        pl.semaphore_signal(barrier, inc=1, device_id={"seq": me + 1}, device_id_type=MESH)

    loads[0].wait()
    bins = bins_ref[...]
    high = (bins >> 7).astype(f32).astype(bf16)
    low = (bins & 127).astype(f32).astype(bf16)
    key_i = lax.broadcasted_iota(jnp.int32, (shard, shard), 0)
    key_j = lax.broadcasted_iota(jnp.int32, (shard, shard), 1)
    lower = jnp.where(key_i >= key_j, 1.0, 0.0).astype(bf16)
    upper = jnp.where(key_i <= key_j, 1.0, 0.0).astype(bf16)
    bcol[...] = 128.0 * mm_nt(lower, high) + mm_nt(lower, low)
    brow[...] = 128.0 * mm(high, upper) + mm(low, upper)

    starts = []
    start = jnp.int32(0)
    for d in range(lengths_ref.shape[0]):
        starts.append(start)
        start = start + lengths_ref[d]

    def doc_of(pos):
        count = jnp.zeros_like(pos)
        for s in starts:
            count = count + jnp.where(pos >= s, 1, 0)
        return count

    key_pos = lax.broadcasted_iota(jnp.int32, (1, shard), 1)
    key_doc = doc_of(first + key_pos)
    query_doc = doc_of(first + row_start + lax.broadcasted_iota(jnp.int32, (1, rows), 1))
    column_doc = doc_of(first + row_start + lax.broadcasted_iota(jnp.int32, (rows, 1), 0))
    one = jnp.zeros((1, 1), jnp.int32)
    prior_doc = doc_of(one + (first - 1))
    before_doc = doc_of(one + (first + row_start - 1))
    end_doc = doc_of(one + (first + shard - 1))
    si = lax.broadcasted_iota(jnp.int32, (rows, rows), 0)
    ti = lax.broadcasted_iota(jnp.int32, (rows, rows), 1)
    penalty[...] = jnp.where((si <= ti) & (column_doc == query_doc), 0.0, FAR)
    end_keep = jnp.where(key_doc == end_doc, 1.0, 0.0)
    shard_keep = jnp.where(end_doc == prior_doc, 1.0, 0.0)
    early_keep = jnp.where(
        (key_doc[:, :rows] == before_doc) & (key_pos[:, :rows] < row_start), 1.0, 0.0
    )
    start_keep = jnp.where(before_doc == prior_doc, 1.0, 0.0)
    carried_keep = jnp.where(query_doc == before_doc, 1.0, 0.0)
    later_core = jnp.where(one + core > 0, 1.0, 0.0)

    def rate_of(h):
        return rates_ref[h] * (-1.0 / total_tokens)

    def lanes(h):
        return pl.ds(pl.multiple_of(h * width, width), width)

    def chain_decay(h):
        return shard_keep * jnp.exp(rate_of(h) * brow[pl.ds(h, 1), :][:, shard - 1 :])

    def forward(src, dst, sent, got, i):
        return pltpu.make_async_remote_copy(
            src_ref=src.at[i], dst_ref=dst.at[core * half + i],
            send_sem=sent.at[i], recv_sem=got.at[i],
            device_id={"seq": jnp.minimum(me + 1, seq_size - 1)}, device_id_type=MESH,
        )

    def across(buf, sent, got, i):
        h = core * half + i
        return pltpu.make_async_remote_copy(
            src_ref=buf.at[h], dst_ref=buf.at[h],
            send_sem=sent.at[i], recv_sem=got.at[i],
            device_id={"sub": 1 - core}, device_id_type=MESH,
        )

    def across_in(buf, sent, got, i):
        h = (1 - core) * half + i
        return pltpu.make_async_remote_copy(
            src_ref=buf.at[h], dst_ref=buf.at[h],
            send_sem=sent.at[i], recv_sem=got.at[i],
            device_id={"sub": 1 - core}, device_id_type=MESH,
        )

    wi = lax.broadcasted_iota(jnp.int32, (width, width), 0)
    wj = lax.broadcasted_iota(jnp.int32, (width, width), 1)
    upper_part = jnp.where(wi <= wj, 1, 0)
    diagonal = wi == wj

    def pieces(k):
        end = width + 8 if k % 3 == 0 else width
        return ((0, width // 2), (width // 2, end))

    def forward(k, n):
        low_row, high_row = pieces(k)[n]
        at = pl.ds(low_row, high_row - low_row)
        return pltpu.make_async_remote_copy(
            src_ref=flow.at[k, at], dst_ref=came.at[core, k, at],
            send_sem=sent.at[k, n], recv_sem=got.at[k, n],
            device_id={"seq": jnp.minimum(me + 1, seq_size - 1)}, device_id_type=MESH,
        )

    def arrival(k, n):
        low_row, high_row = pieces(k)[n]
        at = pl.ds(low_row, high_row - low_row)
        return pltpu.make_async_remote_copy(
            src_ref=flow.at[k, at], dst_ref=came.at[core, k, at],
            send_sem=sent.at[k, n], recv_sem=got.at[k, n],
            device_id={"seq": jnp.maximum(me - 1, 0)}, device_id_type=MESH,
        )

    def across(owner, k, n):
        low_row, high_row = pieces(k)[n]
        at = pl.ds(low_row, high_row - low_row)
        return pltpu.make_async_remote_copy(
            src_ref=came.at[owner, k, at], dst_ref=came.at[owner, k, at],
            send_sem=pass_s.at[k, n], recv_sem=pass_r.at[k, n],
            device_id={"sub": 1 - core}, device_id_type=MESH,
        )

    def own_sums(i):
        h = core * half + i
        sums = brow[pl.ds(h, 1), :]
        weight = end_keep * jnp.exp(rate_of(h) * (sums[:, shard - 1 :] - sums))
        keys = k_ref[:, lanes(h)]
        hi, lo = split(keys.T.astype(f32) * weight)
        both = jnp.concatenate([keys, v_ref[:, lanes(h)]], axis=1)
        total = mm(hi, both) + mm(lo, both)
        k = 3 * (i // 2)
        flow[k + 1 + i % 2, 0:width] = total[:, width:]
        return total[:, :width]

    def own_pair(p):
        one_gram = own_sums(2 * p)
        two_gram = own_sums(2 * p + 1)
        flow[3 * p, 0:width] = jnp.where(wi <= wj, one_gram, two_gram)
        flow[3 * p, width : width + 8] = jnp.broadcast_to(
            jnp.sum(jnp.where(diagonal, two_gram, 0.0), axis=0, keepdims=True), (8, width)
        )

    def source_send(k):
        @pl.when(jnp.logical_not(has_prev) & has_next)
        def _():
            for n in range(2):
                forward(k, n).start()

    def chain_step(k):
        h = core * half + 2 * (k // 3)

        @pl.when(has_prev)
        def _():
            for n in range(2):
                low_row, high_row = pieces(k)[n]
                arrival(k, n).wait_recv()

                @pl.when(has_next)
                def _():
                    if k % 3 == 0:
                        one_decay, two_decay = chain_decay(h), chain_decay(h + 1)
                        decay = jnp.where(
                            wi[low_row:width] <= wj[low_row:width], one_decay, two_decay
                        )
                        decay = jnp.concatenate(
                            [decay, jnp.broadcast_to(two_decay, (8, width))], axis=0
                        )[: high_row - low_row]
                    else:
                        decay = chain_decay(h + k % 3 - 1)
                    flow[k, low_row:high_row] = (
                        decay * came[core, k, low_row:high_row] + flow[k, low_row:high_row]
                    )
                    forward(k, n).start()

                across(core, k, n).start()

    @pl.when(jnp.logical_not(has_prev))
    def _():
        came[...] = jnp.zeros_like(came)

    for load in loads[1:9]:
        load.wait()
    own_pair(0)
    pl.semaphore_wait(
        barrier, 1 + jnp.where(has_prev, 1, 0) + jnp.where(has_next, 1, 0)
    )
    source_send(0)
    for p in range(1, half // 2):
        own_pair(p)
    source_send(1)
    for load in loads[9:]:
        load.wait()

    head_lane = lax.broadcasted_iota(jnp.int32, (rows, heads), 1)

    def query_sums_of(h):
        sums = brow[pl.ds(h, 1), :]
        query_sums = jnp.where(core > 0, sums[:, shard - rows :], sums[:, :rows])
        before = later_core * sums[:, rows - 1 : rows]
        return sums, query_sums, before

    def prepare(i):
        for h in (i, half + i):
            rate = rate_of(h)
            sums, query_sums, before = query_sums_of(h)
            column = jnp.sum(
                jnp.where(head_lane == h, bcol[pl.ds(row_start, rows), :], 0.0),
                axis=1, keepdims=True,
            )
            weight_s[h] = jnp.exp(rate * (query_sums - column) - penalty[...])
            early = early_keep * jnp.exp(
                rate * jnp.maximum(before - sums[:, :rows], 0.0)
            )
            old_keys = k_ref[0:rows, lanes(h)]
            hi, lo = split(old_keys.T.astype(f32) * early)
            both = jnp.concatenate([old_keys, v_ref[0:rows, lanes(h)]], axis=1)
            local = mm(hi, both) + mm(lo, both)
            local_g[h] = local[:, :width]
            local_m[h] = local[:, width:]
            keys_ts[h] = k_ref[pl.ds(row_start, rows), lanes(h)].T
            values_ts[h] = v_ref[pl.ds(row_start, rows), lanes(h)].T
            query_ts[h] = q_ref[:, lanes(h)].T

    ahead = jnp.minimum(half, me * 2)

    def prepare_ahead(i, carry):
        prepare(i)
        return carry

    lax.fori_loop(0, ahead, prepare_ahead, 0)
    chain_step(0)

    def await_other(k, when):
        @pl.when(has_prev & when)
        def _():
            for n in range(2):
                across(1 - core, k, n).wait_recv()

    def pair(i, carry):
        parity = i % 2

        @pl.when(i >= ahead)
        def _():
            prepare(i)

        def source_spot(spot):
            for k in range(2, steps):
                if (k - 2) % 3 == spot:
                    pl.when(i == (k - 2) // 3)(functools.partial(source_send, k))

        source_spot(0)
        for k in range(0, steps, 3):
            await_other(k, i == 2 * (k // 3))

        group = (i, half + i)
        state = []
        for owner, h in enumerate(group):
            rate = rate_of(h)
            sums, query_sums, before = query_sums_of(h)
            carried = carried_keep * jnp.exp(rate * (query_sums - before))
            decay = start_keep * jnp.exp(rate * before)
            packed = came[owner, 3 * (i // 2)]
            square = packed[:width]
            gram = jnp.where(upper_part != parity, square, square.T)
            gram = jnp.where(diagonal & (parity == 1), packed[width : width + 1], gram)
            ghi, glo = split(decay * gram + local_g[h])
            keys = k_ref[pl.ds(row_start, rows), lanes(h)]
            left = jnp.concatenate(
                [
                    jnp.concatenate([keys, keys], axis=1),
                    jnp.concatenate([ghi, ghi], axis=1),
                    jnp.concatenate([glo, glo], axis=1),
                ],
                axis=0,
            )
            query = query_ts[h].astype(f32)
            state.append(
                dict(
                    h=h, carried=carried, decay=decay,
                    left=left, ridge=ridge_ref[h],
                    x=jnp.zeros_like(query), r=query, p=query,
                    energy=jnp.sum(query * query, axis=0, keepdims=True),
                )
            )
        for iteration in range(ITERS):
            for s in state:
                hi, lo = split(s["p"])
                s["y"] = mm(s["left"], jnp.concatenate([hi, lo], axis=0))
            for s in state:
                hi, lo = split(s["y"][:rows] * weight_s[s["h"]])
                a = mm(keys_ts[s["h"]], hi) + mm(keys_ts[s["h"]], lo)
                earlier = s["y"][rows : rows + width] + s["y"][rows + width :]
                s["a"] = s["carried"] * earlier + a + s["ridge"] * s["p"]
            for s in state:
                p, a = s["p"], s["a"]
                alpha = s["energy"] / (jnp.sum(p * a, axis=0, keepdims=True) + GUARD)
                s["x"] = s["x"] + alpha * p
                if iteration < ITERS - 1:
                    r = s["r"] - alpha * a
                    energy = jnp.sum(r * r, axis=0, keepdims=True)
                    s["p"] = r + (energy / (s["energy"] + GUARD)) * p
                    s["r"], s["energy"] = r, energy
            if iteration % 2 == 1:
                spot = iteration // 2
                source_spot(spot + 1)
                for k in range(1, steps):
                    if (k - 1) % 2 == spot:
                        pl.when(i == (k - 1) // 2)(functools.partial(chain_step, k))

        within = []
        for h, s in zip(group, state):
            hi, lo = split(s["x"])
            s["hilo"] = jnp.concatenate([hi, lo], axis=0)
            keys2 = s["left"][:rows]
            hi, lo = split(mm(keys2, s["hilo"]) * weight_s[h])
            within.append(mm(values_ts[h], hi) + mm(values_ts[h], lo))

        for k in range(steps):
            if k % 3 > 0:
                await_other(k, i == 2 * (k // 3) + k % 3 - 1)
        for owner, (h, s, inner) in enumerate(zip(group, state, within)):
            memory = came[owner, 3 * (i // 2) + 1 + parity][:width]
            mhi, mlo = split((s["decay"] * memory + local_m[h]).T)
            left = jnp.concatenate(
                [
                    jnp.concatenate([mhi, mhi], axis=1),
                    jnp.concatenate([mlo, mlo], axis=1),
                ],
                axis=0,
            )
            y = mm(left, s["hilo"])
            out = s["carried"] * (y[:width] + y[width:]) + inner
            out_ref[:, lanes(h)] = out.T.astype(bf16)
        return carry

    lax.fori_loop(0, half, pair, 0)

    @pl.when(has_prev)
    def _():
        for k in range(steps):
            for n in range(2):
                across(core, k, n).wait_send()

    @pl.when(has_next)
    def _():
        for k in range(steps):
            for n in range(2):
                forward(k, n).wait_send()


def per_device(seq_size, queries, keys, values, gate_bins, doc_lengths, decay_rates, ridge_terms):
    heads = decay_rates.shape[0]
    rows = queries.shape[0]
    shard = keys.shape[0]
    half = heads // 2
    steps = 3 * (half // 2)
    width = keys.shape[1] // heads
    smem = pl.BlockSpec(memory_space=pltpu.SMEM)
    vmem = pl.BlockSpec(memory_space=pltpu.VMEM)
    hbm = pl.BlockSpec(memory_space=pltpu.HBM)
    square = pltpu.VMEM((heads, width, width), f32)
    turned = pltpu.VMEM((heads, width, rows), bf16)
    flops = 2 * heads * rows * 256 * 768 * 5
    return pl.pallas_call(
        functools.partial(kernel, seq_size, heads, rows, shard * seq_size),
        out_shape=jax.ShapeDtypeStruct(queries.shape, bf16),
        in_specs=[smem, smem, smem, hbm, hbm, hbm, hbm],
        out_specs=vmem,
        scratch_shapes=[
            pltpu.VMEM(queries.shape, bf16),
            pltpu.VMEM(keys.shape, bf16),
            pltpu.VMEM(values.shape, bf16),
            pltpu.VMEM((heads, shard), jnp.int32),
            pltpu.VMEM((shard, heads), f32),
            pltpu.VMEM((heads, shard), f32),
            pltpu.VMEM((rows, rows), f32),
            pltpu.VMEM((2, steps, width + 8, width), f32),
            pltpu.VMEM((steps, width + 8, width), f32),
            pltpu.VMEM((heads, rows, rows), f32),
            square, square, turned, turned, turned,
        ] + [pltpu.SemaphoreType.DMA((steps, 2))] * 4 + [pltpu.SemaphoreType.DMA((16,))],
        compiler_params=pltpu.CompilerParams(
            collective_id=0, has_side_effects=True, vmem_limit_bytes=62 * 1024 * 1024
        ),
        cost_estimate=pl.CostEstimate(
            flops=flops, bytes_accessed=4 * 1024 * 1024, transcendentals=heads * rows * rows
        ),
    )(doc_lengths, decay_rates, ridge_terms, queries, keys, values, gate_bins.T)


def solution(mesh):
    in_specs = (
        P(("rep", "seq", "sub"), "head"),
        P(("rep", "seq"), "head"),
        P(("rep", "seq"), "head"),
        P(("rep", "seq"), "head"),
        P("rep"),
        P("head"),
        P("head"),
    )
    out_specs = P(("rep", "seq", "sub"), "head")
    return jax.shard_map(
        functools.partial(per_device, mesh.shape["seq"]),
        mesh=mesh, in_specs=in_specs, out_specs=out_specs, check_vma=False,
    )
```

```python
import functools

import jax
import jax.numpy as jnp
from jax import lax
from jax.experimental import pallas as pl
from jax.experimental.pallas import tpu as pltpu
from jax.sharding import PartitionSpec as P

ITERS = 4
GUARD = 1e-06
FAR = 1e30
MESH = pl.DeviceIdType.MESH
f32 = jnp.float32
bf16 = jnp.bfloat16


def mm(a, b):
    return jnp.dot(a, b, preferred_element_type=f32)


def mm_nt(a, b):
    return lax.dot_general(a, b, (((1,), (1,)), ((), ())), preferred_element_type=f32)


def split(x):
    hi = x.astype(bf16)
    return hi, (x - hi.astype(f32)).astype(bf16)


def kernel(
    seq_size, heads, rows, total_tokens,
    lengths_ref, rates_ref, ridge_ref, q_hbm, k_hbm, v_hbm, bins_hbm, out_ref,
    q_ref, k_ref, v_ref, bins_ref,
    bcol, brow, penalty, came, flow,
    weight_s, local_g, local_m, keys_ts, values_ts, query_ts,
    sent, got, pass_s, pass_r, load_sem,
):
    shard = k_ref.shape[0]
    half = heads // 2
    width = came.shape[3]
    steps = flow.shape[0]
    me = lax.axis_index("seq")
    core = lax.axis_index("sub")
    row_start = pl.multiple_of(core * rows, rows)
    first = me * shard
    has_prev = me > 0
    has_next = me < seq_size - 1

    loads = [(bins_hbm, bins_ref)]
    piece = shard // 4
    for src, dst in ((k_hbm, k_ref), (v_hbm, v_ref), (q_hbm, q_ref)):
        for at in range(0, src.shape[0], piece):
            loads.append((src.at[pl.ds(at, piece)], dst.at[pl.ds(at, piece)]))
    loads = [
        pltpu.make_async_copy(src, dst, load_sem.at[at]) for at, (src, dst) in enumerate(loads)
    ]
    for load in loads:
        load.start()

    barrier = pltpu.get_barrier_semaphore()
    pl.semaphore_signal(barrier, inc=1, device_id={"sub": 1 - core}, device_id_type=MESH)

    @pl.when(has_prev)
    def _():
        pl.semaphore_signal(barrier, inc=1, device_id={"seq": me - 1}, device_id_type=MESH)

    @pl.when(has_next)
    def _():
        pl.semaphore_signal(barrier, inc=1, device_id={"seq": me + 1}, device_id_type=MESH)

    loads[0].wait()
    bins = bins_ref[...]
    high = (bins >> 7).astype(f32).astype(bf16)
    low = (bins & 127).astype(f32).astype(bf16)
    key_i = lax.broadcasted_iota(jnp.int32, (shard, shard), 0)
    key_j = lax.broadcasted_iota(jnp.int32, (shard, shard), 1)
    lower = jnp.where(key_i >= key_j, 1.0, 0.0).astype(bf16)
    upper = jnp.where(key_i <= key_j, 1.0, 0.0).astype(bf16)
    bcol[...] = 128.0 * mm_nt(lower, high) + mm_nt(lower, low)
    brow[...] = 128.0 * mm(high, upper) + mm(low, upper)

    starts = []
    start = jnp.int32(0)
    for d in range(lengths_ref.shape[0]):
        starts.append(start)
        start = start + lengths_ref[d]

    def doc_of(pos):
        count = jnp.zeros_like(pos)
        for s in starts:
            count = count + jnp.where(pos >= s, 1, 0)
        return count

    key_pos = lax.broadcasted_iota(jnp.int32, (1, shard), 1)
    key_doc = doc_of(first + key_pos)
    query_doc = doc_of(first + row_start + lax.broadcasted_iota(jnp.int32, (1, rows), 1))
    column_doc = doc_of(first + row_start + lax.broadcasted_iota(jnp.int32, (rows, 1), 0))
    one = jnp.zeros((1, 1), jnp.int32)
    prior_doc = doc_of(one + (first - 1))
    before_doc = doc_of(one + (first + row_start - 1))
    end_doc = doc_of(one + (first + shard - 1))
    si = lax.broadcasted_iota(jnp.int32, (rows, rows), 0)
    ti = lax.broadcasted_iota(jnp.int32, (rows, rows), 1)
    penalty[...] = jnp.where((si <= ti) & (column_doc == query_doc), 0.0, FAR)
    end_keep = jnp.where(key_doc == end_doc, 1.0, 0.0)
    shard_keep = jnp.where(end_doc == prior_doc, 1.0, 0.0)
    early_keep = jnp.where(
        (key_doc[:, :rows] == before_doc) & (key_pos[:, :rows] < row_start), 1.0, 0.0
    )
    start_keep = jnp.where(before_doc == prior_doc, 1.0, 0.0)
    carried_keep = jnp.where(query_doc == before_doc, 1.0, 0.0)
    later_core = jnp.where(one + core > 0, 1.0, 0.0)

    def rate_of(h):
        return rates_ref[h] * (-1.0 / total_tokens)

    def lanes(h):
        return pl.ds(pl.multiple_of(h * width, width), width)

    def chain_decay(h):
        return shard_keep * jnp.exp(rate_of(h) * brow[pl.ds(h, 1), :][:, shard - 1 :])

    def forward(src, dst, sent, got, i):
        return pltpu.make_async_remote_copy(
            src_ref=src.at[i], dst_ref=dst.at[core * half + i],
            send_sem=sent.at[i], recv_sem=got.at[i],
            device_id={"seq": jnp.minimum(me + 1, seq_size - 1)}, device_id_type=MESH,
        )

    def across(buf, sent, got, i):
        h = core * half + i
        return pltpu.make_async_remote_copy(
            src_ref=buf.at[h], dst_ref=buf.at[h],
            send_sem=sent.at[i], recv_sem=got.at[i],
            device_id={"sub": 1 - core}, device_id_type=MESH,
        )

    def across_in(buf, sent, got, i):
        h = (1 - core) * half + i
        return pltpu.make_async_remote_copy(
            src_ref=buf.at[h], dst_ref=buf.at[h],
            send_sem=sent.at[i], recv_sem=got.at[i],
            device_id={"sub": 1 - core}, device_id_type=MESH,
        )

    wi = lax.broadcasted_iota(jnp.int32, (width, width), 0)
    wj = lax.broadcasted_iota(jnp.int32, (width, width), 1)
    upper_part = jnp.where(wi <= wj, 1, 0)
    diagonal = wi == wj

    def pieces(k):
        end = width + 8 if k % 3 == 0 else width
        return ((0, width // 2), (width // 2, end))

    def forward(k, n):
        low_row, high_row = pieces(k)[n]
        at = pl.ds(low_row, high_row - low_row)
        return pltpu.make_async_remote_copy(
            src_ref=flow.at[k, at], dst_ref=came.at[core, k, at],
            send_sem=sent.at[k, n], recv_sem=got.at[k, n],
            device_id={"seq": jnp.minimum(me + 1, seq_size - 1)}, device_id_type=MESH,
        )

    def arrival(k, n):
        low_row, high_row = pieces(k)[n]
        at = pl.ds(low_row, high_row - low_row)
        return pltpu.make_async_remote_copy(
            src_ref=flow.at[k, at], dst_ref=came.at[core, k, at],
            send_sem=sent.at[k, n], recv_sem=got.at[k, n],
            device_id={"seq": jnp.maximum(me - 1, 0)}, device_id_type=MESH,
        )

    def across(owner, k, n):
        low_row, high_row = pieces(k)[n]
        at = pl.ds(low_row, high_row - low_row)
        return pltpu.make_async_remote_copy(
            src_ref=came.at[owner, k, at], dst_ref=came.at[owner, k, at],
            send_sem=pass_s.at[k, n], recv_sem=pass_r.at[k, n],
            device_id={"sub": 1 - core}, device_id_type=MESH,
        )

    def own_sums(i):
        h = core * half + i
        sums = brow[pl.ds(h, 1), :]
        weight = end_keep * jnp.exp(rate_of(h) * (sums[:, shard - 1 :] - sums))
        keys = k_ref[:, lanes(h)]
        hi, lo = split(keys.T.astype(f32) * weight)
        both = jnp.concatenate([keys, v_ref[:, lanes(h)]], axis=1)
        total = mm(hi, both) + mm(lo, both)
        k = 3 * (i // 2)
        flow[k + 1 + i % 2, 0:width] = total[:, width:]
        return total[:, :width]

    def own_pair(p):
        one_gram = own_sums(2 * p)
        two_gram = own_sums(2 * p + 1)
        flow[3 * p, 0:width] = jnp.where(wi <= wj, one_gram, two_gram)
        flow[3 * p, width : width + 8] = jnp.broadcast_to(
            jnp.sum(jnp.where(diagonal, two_gram, 0.0), axis=0, keepdims=True), (8, width)
        )

    def source_send(k):
        @pl.when(jnp.logical_not(has_prev) & has_next)
        def _():
            for n in range(2):
                forward(k, n).start()

    def chain_step(k):
        h = core * half + 2 * (k // 3)

        @pl.when(has_prev)
        def _():
            for n in range(2):
                low_row, high_row = pieces(k)[n]
                arrival(k, n).wait_recv()

                @pl.when(has_next)
                def _():
                    if k % 3 == 0:
                        one_decay, two_decay = chain_decay(h), chain_decay(h + 1)
                        decay = jnp.where(
                            wi[low_row:width] <= wj[low_row:width], one_decay, two_decay
                        )
                        decay = jnp.concatenate(
                            [decay, jnp.broadcast_to(two_decay, (8, width))], axis=0
                        )[: high_row - low_row]
                    else:
                        decay = chain_decay(h + k % 3 - 1)
                    flow[k, low_row:high_row] = (
                        decay * came[core, k, low_row:high_row] + flow[k, low_row:high_row]
                    )
                    forward(k, n).start()

                across(core, k, n).start()

    @pl.when(jnp.logical_not(has_prev))
    def _():
        came[...] = jnp.zeros_like(came)

    for load in loads[1:9]:
        load.wait()
    own_pair(0)
    pl.semaphore_wait(
        barrier, 1 + jnp.where(has_prev, 1, 0) + jnp.where(has_next, 1, 0)
    )
    source_send(0)
    for p in range(1, half // 2):
        own_pair(p)
    source_send(1)
    for load in loads[9:]:
        load.wait()

    head_lane = lax.broadcasted_iota(jnp.int32, (rows, heads), 1)

    def query_sums_of(h):
        sums = brow[pl.ds(h, 1), :]
        query_sums = jnp.where(core > 0, sums[:, shard - rows :], sums[:, :rows])
        before = later_core * sums[:, rows - 1 : rows]
        return sums, query_sums, before

    def prepare(i):
        for h in (i, half + i):
            rate = rate_of(h)
            sums, query_sums, before = query_sums_of(h)
            column = jnp.sum(
                jnp.where(head_lane == h, bcol[pl.ds(row_start, rows), :], 0.0),
                axis=1, keepdims=True,
            )
            weight_s[h] = jnp.exp(rate * (query_sums - column) - penalty[...])
            early = early_keep * jnp.exp(
                rate * jnp.maximum(before - sums[:, :rows], 0.0)
            )
            old_keys = k_ref[0:rows, lanes(h)]
            hi, lo = split(old_keys.T.astype(f32) * early)
            both = jnp.concatenate([old_keys, v_ref[0:rows, lanes(h)]], axis=1)
            local = mm(hi, both) + mm(lo, both)
            local_g[h] = local[:, :width]
            local_m[h] = local[:, width:]
            keys_ts[h] = k_ref[pl.ds(row_start, rows), lanes(h)].T
            values_ts[h] = v_ref[pl.ds(row_start, rows), lanes(h)].T
            query_ts[h] = q_ref[:, lanes(h)].T

    ahead = jnp.minimum(half, me * 2)

    def prepare_ahead(i, carry):
        prepare(i)
        return carry

    lax.fori_loop(0, ahead, prepare_ahead, 0)
    chain_step(0)

    def await_other(k, when):
        @pl.when(has_prev & when)
        def _():
            for n in range(2):
                across(1 - core, k, n).wait_recv()

    def pair(i, carry):
        parity = i % 2

        @pl.when(i >= ahead)
        def _():
            prepare(i)

        def source_spot(spot):
            for k in range(2, steps):
                if (k - 2) % 3 == spot:
                    pl.when(i == (k - 2) // 3)(functools.partial(source_send, k))

        source_spot(0)
        for k in range(0, steps, 3):
            await_other(k, i == 2 * (k // 3))

        group = (i, half + i)
        state = []
        for owner, h in enumerate(group):
            rate = rate_of(h)
            sums, query_sums, before = query_sums_of(h)
            carried = carried_keep * jnp.exp(rate * (query_sums - before))
            decay = start_keep * jnp.exp(rate * before)
            packed = came[owner, 3 * (i // 2)]
            square = packed[:width]
            gram = jnp.where(upper_part != parity, square, square.T)
            gram = jnp.where(diagonal & (parity == 1), packed[width : width + 1], gram)
            ghi, glo = split(decay * gram + local_g[h])
            keys = k_ref[pl.ds(row_start, rows), lanes(h)]
            left = jnp.concatenate(
                [
                    jnp.concatenate([keys, keys], axis=1),
                    jnp.concatenate([ghi, ghi], axis=1),
                    jnp.concatenate([glo, glo], axis=1),
                ],
                axis=0,
            )
            query = query_ts[h].astype(f32)
            state.append(
                dict(
                    h=h, carried=carried, decay=decay,
                    left=left, ridge=ridge_ref[h],
                    x=jnp.zeros_like(query), r=query, p=query,
                    energy=jnp.sum(query * query, axis=0, keepdims=True),
                )
            )
        for iteration in range(ITERS):
            for s in state:
                hi, lo = split(s["p"])
                s["y"] = mm(s["left"], jnp.concatenate([hi, lo], axis=0))
            for s in state:
                hi, lo = split(s["y"][:rows] * weight_s[s["h"]])
                a = mm(keys_ts[s["h"]], hi) + mm(keys_ts[s["h"]], lo)
                earlier = s["y"][rows : rows + width] + s["y"][rows + width :]
                s["a"] = s["carried"] * earlier + a + s["ridge"] * s["p"]
            for s in state:
                p, a = s["p"], s["a"]
                alpha = s["energy"] / (jnp.sum(p * a, axis=0, keepdims=True) + GUARD)
                s["x"] = s["x"] + alpha * p
                if iteration < ITERS - 1:
                    r = s["r"] - alpha * a
                    energy = jnp.sum(r * r, axis=0, keepdims=True)
                    s["p"] = r + (energy / (s["energy"] + GUARD)) * p
                    s["r"], s["energy"] = r, energy
            if iteration % 2 == 1:
                source_spot(iteration // 2 + 1)
            for k in range(1, steps):
                early_at, late_at = k - 1, 2 * k - 1
                if early_at % ITERS == iteration:
                    pl.when((i == early_at // ITERS) & has_next)(
                        functools.partial(chain_step, k)
                    )
                if late_at % ITERS == iteration:
                    pl.when((i == late_at // ITERS) & jnp.logical_not(has_next))(
                        functools.partial(chain_step, k)
                    )

        within = []
        for h, s in zip(group, state):
            hi, lo = split(s["x"])
            s["hilo"] = jnp.concatenate([hi, lo], axis=0)
            keys2 = s["left"][:rows]
            hi, lo = split(mm(keys2, s["hilo"]) * weight_s[h])
            within.append(mm(values_ts[h], hi) + mm(values_ts[h], lo))

        for k in range(steps):
            if k % 3 > 0:
                await_other(k, i == 2 * (k // 3) + k % 3 - 1)
        for owner, (h, s, inner) in enumerate(zip(group, state, within)):
            memory = came[owner, 3 * (i // 2) + 1 + parity][:width]
            mhi, mlo = split((s["decay"] * memory + local_m[h]).T)
            left = jnp.concatenate(
                [
                    jnp.concatenate([mhi, mhi], axis=1),
                    jnp.concatenate([mlo, mlo], axis=1),
                ],
                axis=0,
            )
            y = mm(left, s["hilo"])
            out = s["carried"] * (y[:width] + y[width:]) + inner
            out_ref[:, lanes(h)] = out.T.astype(bf16)
        return carry

    lax.fori_loop(0, half, pair, 0)

    @pl.when(has_prev)
    def _():
        for k in range(steps):
            for n in range(2):
                across(core, k, n).wait_send()

    @pl.when(has_next)
    def _():
        for k in range(steps):
            for n in range(2):
                forward(k, n).wait_send()


def per_device(seq_size, queries, keys, values, gate_bins, doc_lengths, decay_rates, ridge_terms):
    heads = decay_rates.shape[0]
    rows = queries.shape[0]
    shard = keys.shape[0]
    half = heads // 2
    steps = 3 * (half // 2)
    width = keys.shape[1] // heads
    smem = pl.BlockSpec(memory_space=pltpu.SMEM)
    vmem = pl.BlockSpec(memory_space=pltpu.VMEM)
    hbm = pl.BlockSpec(memory_space=pltpu.HBM)
    square = pltpu.VMEM((heads, width, width), f32)
    turned = pltpu.VMEM((heads, width, rows), bf16)
    flops = 2 * heads * rows * 256 * 768 * 5
    return pl.pallas_call(
        functools.partial(kernel, seq_size, heads, rows, shard * seq_size),
        out_shape=jax.ShapeDtypeStruct(queries.shape, bf16),
        in_specs=[smem, smem, smem, hbm, hbm, hbm, hbm],
        out_specs=vmem,
        scratch_shapes=[
            pltpu.VMEM(queries.shape, bf16),
            pltpu.VMEM(keys.shape, bf16),
            pltpu.VMEM(values.shape, bf16),
            pltpu.VMEM((heads, shard), jnp.int32),
            pltpu.VMEM((shard, heads), f32),
            pltpu.VMEM((heads, shard), f32),
            pltpu.VMEM((rows, rows), f32),
            pltpu.VMEM((2, steps, width + 8, width), f32),
            pltpu.VMEM((steps, width + 8, width), f32),
            pltpu.VMEM((heads, rows, rows), f32),
            square, square, turned, turned, turned,
        ] + [pltpu.SemaphoreType.DMA((steps, 2))] * 4 + [pltpu.SemaphoreType.DMA((16,))],
        compiler_params=pltpu.CompilerParams(
            collective_id=0, has_side_effects=True, vmem_limit_bytes=53 * 1024 * 1024
        ),
        cost_estimate=pl.CostEstimate(
            flops=flops, bytes_accessed=4 * 1024 * 1024, transcendentals=heads * rows * rows
        ),
    )(doc_lengths, decay_rates, ridge_terms, queries, keys, values, gate_bins.T)


def solution(mesh):
    in_specs = (
        P(("rep", "seq", "sub"), "head"),
        P(("rep", "seq"), "head"),
        P(("rep", "seq"), "head"),
        P(("rep", "seq"), "head"),
        P("rep"),
        P("head"),
        P("head"),
    )
    out_specs = P(("rep", "seq", "sub"), "head")
    return jax.shard_map(
        functools.partial(per_device, mesh.shape["seq"]),
        mesh=mesh, in_specs=in_specs, out_specs=out_specs, check_vma=False,
    )
```
